128 devices in a mesh: box: 32 (over x, z, core), grp: 4 (over y).
Axes of the slice: x: 4, y: 4, z: 4, core: 2. Of those that a mesh axis runs over, the one named last changes fastest.
Arguments:
- coupling: bfloat16 [512, 256, 768], P(('box', 'grp')), may hold values from -1.1953125 to 1.1953125
- inverse: bfloat16 [512, 768, 768], P(('box', 'grp')), may hold values from -0.21875 to 0.21875
- tiles: bfloat16 [512, 6, 768, 256], P(('box', 'grp')), may hold values from -1.1953125 to 1.1953125
- near_block: bfloat16 [512, 256, 1792], P(('box', 'grp')), may hold values from -3 to 3
- neighbour: int32 [512, 6], P(('box', 'grp')), may hold values from 0 to 511, as said below
- source_slot: int32 [512, 6], P(('box', 'grp')), may hold values from 0 to 5
Outputs:
- updated: bfloat16 [512, 256, 1792], P('grp', 'box')
The draws below stay inside these ranges and needn't reach their ends.
Inputs may be any that keep to these rules, and one draw needn't show every extreme that they name: `neighbour`: the box storing a slot's tile lies on the device holding the box, or on the device just before or after it in the order of box+grp, cyclically. Every tile is read by exactly one slot of one box. Between two adjacent devices as many tiles are read in one direction as in the other, at most 12, and exactly 12 between some pair of devices.
All inputs are finite; a program needn't handle non-finite values.
Results may differ from the reference program's by a relative error of at most 0.008.
Values may be sent and summed in bfloat16 or wider, within the bound.
A program may use at most 128 MiB of HBM per device.

```python
import jax
import jax.numpy as jnp
from jax import lax

SKEL = 256
REDUND = 768
NEIGH = 6
BOX_DEV = 4
FAR = 12
BOXES = 512


def pairing(key):
    device_count = BOXES // BOX_DEV
    per_device = BOX_DEV * NEIGH
    key_links, key_order, key_store = jax.random.split(key, 3)
    links = jax.random.randint(key_links, (device_count,), 1, FAR + 1).astype(jnp.int32)
    links = links.at[0].set(FAR)

    def shuffled(one_key):
        return jax.random.permutation(one_key, per_device).astype(jnp.int32)
    order = jax.vmap(shuffled)(jax.random.split(key_order, device_count))
    store = jax.vmap(shuffled)(jax.random.split(key_store, device_count))
    device_ids = jnp.arange(device_count, dtype=jnp.int32)[:, None]
    after_ids = (device_ids + 1) % device_count
    before_ids = (device_ids + device_count - 1) % device_count
    ahead = links[:, None]
    behind = links[before_ids[:, 0]][:, None]
    take_after = order < ahead
    take_before = order >= per_device - behind
    own_place = jnp.clip(order - ahead + behind, 0, per_device - 1)
    slot_after = jnp.take_along_axis(store[after_ids[:, 0]], order, axis=1)
    slot_before = jnp.take_along_axis(store[before_ids[:, 0]], order, axis=1)
    slot_own = jnp.take_along_axis(store, own_place, axis=1)
    source_device = jnp.where(take_after, after_ids, jnp.where(take_before, before_ids, device_ids))
    source_place = jnp.where(take_after, slot_after, jnp.where(take_before, slot_before, slot_own))
    source_box = source_device * BOX_DEV + source_place // NEIGH
    slot_number = source_place % NEIGH
    return (source_box.reshape(BOXES, NEIGH).astype(jnp.int32), slot_number.reshape(BOXES, NEIGH).astype(jnp.int32))


def draw_neighbour(key, part):
    source_box, slot_number = pairing(key)
    return source_box


def draw_source_slot(key, part):
    source_box, slot_number = pairing(key)
    return slot_number


def levels(stream_key, dims, cuts, smallest, top_value):
    gain, own = 1.0, jax.random.fold_in(stream_key, 6)
    for axis_at, blocks in cuts:
        draws = jnp.exp(jax.random.uniform(jax.random.fold_in(own, axis_at), (blocks,), jnp.float32, smallest / len(cuts), top_value / len(cuts)))
        gain = gain * jnp.repeat(draws, dims[axis_at] // blocks).reshape([-1 if axis == axis_at else 1 for axis in range(len(dims))])
    return gain


def centred(own_key, shape, spread, bound, cuts=(), kind=jnp.bfloat16):
    result = spread * jax.random.normal(own_key, shape, jnp.float32)
    if cuts:
        result = result * levels(own_key, shape, cuts, -0.22, 0.18)
    return jnp.clip(result, -bound, bound).astype(kind)


def setup_inputs(seed: int = 0) -> dict:
    key_of = jax.random.split(jax.random.key(seed), 7)
    return {
        "coupling": centred(key_of[0], (BOXES, SKEL, REDUND), 0.19, 1.1953125, ((0, 128),)),
        "inverse": centred(key_of[1], (BOXES, REDUND, REDUND), REDUND ** -0.5, 0.21875, ((0, 128),)),
        "tiles": centred(key_of[2], (BOXES, NEIGH, REDUND, SKEL), 0.19, 1.1953125, ((0, 128),)),
        "near_block": centred(key_of[3], (BOXES, SKEL, (NEIGH + 1) * SKEL), 0.5, 3.0, ((0, 128),)),
        "neighbour": draw_neighbour(jax.random.fold_in(key_of[6], 71), 0),
        "source_slot": draw_source_slot(jax.random.fold_in(key_of[6], 71), 0),
    }


def reference(coupling, inverse, tiles, near_block, neighbour, source_slot):
    tile_rows = tiles.reshape(BOXES * NEIGH, REDUND, SKEL)

    def one_box(items):
        rows, inv_block, near_rows, sources, slots = items
        weights = jnp.dot(rows, inv_block, preferred_element_type=jnp.float32).astype(jnp.bfloat16)
        picked = tile_rows[(sources * NEIGH + slots).astype(jnp.int32)]
        pair_term = jnp.einsum("kr,jrc->kjc", weights.astype(jnp.float32), picked.astype(jnp.float32))
        own_term = jnp.dot(weights, rows.T, preferred_element_type=jnp.float32)
        combined = jnp.concatenate([own_term[:, None, :], pair_term], axis=1).reshape(SKEL, (NEIGH + 1) * SKEL)
        return (near_rows.astype(jnp.float32) - combined).astype(jnp.bfloat16)

    return lax.map(one_box, (coupling, inverse, near_block, neighbour, source_slot))
```

```python
import functools

import jax
import jax.numpy as jnp
from jax import lax
from jax.experimental import pallas as pl
from jax.experimental.pallas import tpu as pltpu
from jax.sharding import PartitionSpec as P

FAR = 12
HALVES = 2
MESH = pl.DeviceIdType.MESH


def request_tables(neighbour, source_slot, device_now, device_count):
    box_count, slot_count = neighbour.shape
    total = box_count * slot_count
    boxes = neighbour.reshape(-1)
    owner = boxes // box_count
    place = (boxes - owner * box_count) * slot_count + source_slot.reshape(-1)
    asked = jnp.stack(
        [
            owner == (device_now + 1) % device_count,
            owner == (device_now + device_count - 1) % device_count,
        ]
    )
    order = jnp.arange(total, dtype=jnp.int32)
    before = (order[None, :] < order[:, None]).astype(jnp.int32)
    rank = jnp.sum(before[None] * asked[:, None, :].astype(jnp.int32), axis=2)
    lanes = jnp.arange(128, dtype=jnp.int32)
    onehot = jnp.logical_and(
        jnp.logical_and(rank[:, None, :] == lanes[None, :, None], lanes[None, :, None] < FAR), asked[:, None, :]
    ).astype(jnp.int32)
    tile_list = jnp.sum(onehot * place[None, None, :], axis=2)
    box_list = jnp.sum(onehot * (order // slot_count)[None, None, :], axis=2)
    lists = jnp.stack([tile_list, box_list] + [jnp.zeros_like(tile_list)] * 6, axis=1)
    here = jnp.logical_not(jnp.logical_or(asked[0], asked[1]))
    local_tile = jnp.where(here, place, total)
    result_at = jnp.where(asked[0], rank[0], jnp.where(asked[1], FAR + rank[1], 2 * FAR))
    return lists, jnp.stack([local_tile, result_at])


def kernel(
    groups, boxes_axis,
    table, lists, split_coupling, coupling, inverse, tiles, split_near,
    out,
    cp, inv, full_c, tile, base, own_w, wr0, wr1, rs0, rs1, res0, res1, ob0, ob1, stage, list_in, list_s,
    load_sem, list_send, list_recv, w_send, w_recv, r_send, r_recv, st_send, st_recv, out_send, out_recv,
):
    box_count, halves, half_rows, red = cp.shape
    skel = halves * half_rows
    slots = 6
    total = box_count * slots
    per_group = boxes_axis // groups
    z_count = per_group // 2
    z_half = z_count // 2
    dests = boxes_axis // 2
    wr, rs, res, ob = (wr0, wr1), (rs0, rs1), (res0, res1), (ob0, ob1)
    b = lax.axis_index("box")
    g = lax.axis_index("grp")
    x = b // per_group
    z = (b % per_group) // 2
    c = b % 2
    count = boxes_axis * groups
    here = b * groups + g
    after = lax.rem(here + 1, count)
    behind = lax.rem(here + count - 1, count)
    near_devices = ((after // groups, after % groups), (behind // groups, behind % groups))
    parity = [lax.rem(z + h, 2) for h in range(halves)]

    barrier = pltpu.get_barrier_semaphore()

    def greet(k, carry):
        pl.semaphore_signal(barrier, inc=1, device_id=(lax.rem(b + k, boxes_axis), g), device_id_type=MESH)
        return carry

    lax.fori_loop(1, boxes_axis, greet, 0)
    for k in range(1, groups):
        pl.semaphore_signal(barrier, inc=1, device_id=(b, lax.rem(g + k, groups)), device_id_type=MESH)
    for device in near_devices:
        pl.semaphore_signal(barrier, inc=1, device_id=device, device_id_type=MESH)

    def load_c(a, h):
        return pltpu.make_async_copy(
            split_coupling.at[a, :, :, parity[h]], cp6.at[a, h], load_sem.at[a * 3 + h]
        )

    cp6 = cp.reshape(box_count, halves, groups, z_half, 16, red)
    near6 = base.reshape(box_count, halves, groups, z_half, 16, base.shape[-1])

    def load_inv(a):
        return pltpu.make_async_copy(inverse.at[a], inv.at[a], load_sem.at[a * 3 + 2])

    for a in range(box_count):
        for h in range(halves):
            load_c(a, h).start()
        load_inv(a).start()
    first = 3 * box_count
    rest = [
        pltpu.make_async_copy(coupling, full_c, load_sem.at[first]),
        pltpu.make_async_copy(tiles, tile.at[pl.ds(0, total)], load_sem.at[first + 1]),
    ] + [
        pltpu.make_async_copy(split_near.at[:, :, :, parity[h]], near6.at[:, h], load_sem.at[first + 2 + h])
        for h in range(halves)
    ]
    for copy in rest:
        copy.start()
    tile[total] = jnp.zeros_like(tile[total])
    for h in range(halves):
        res[h][2 * FAR] = jnp.zeros_like(res[h][2 * FAR])

    pl.semaphore_wait(barrier, boxes_axis - 1 + groups - 1 + 2)

    list_copies = [
        pltpu.make_async_remote_copy(
            src_ref=lists.at[d],
            dst_ref=list_in.at[1 - d],
            send_sem=list_send.at[d],
            recv_sem=list_recv.at[1 - d],
            device_id=near_devices[d],
            device_id_type=MESH,
        )
        for d in range(2)
    ]
    for copy in list_copies:
        copy.start()

    def send_w(a, h):
        for d in range(2):
            pltpu.make_async_remote_copy(
                src_ref=own_w.at[a, h],
                dst_ref=wr[h].at[1 - d, a],
                send_sem=w_send.at[h, d],
                recv_sem=w_recv.at[h, 1 - d],
                device_id=near_devices[d],
                device_id_type=MESH,
            ).start()

    def weights(a, carry):
        for h in range(halves):
            load_c(a, h).wait()
        load_inv(a).wait()
        product = jnp.dot(cp[a].reshape(skel, red), inv[a], preferred_element_type=jnp.float32)
        own_w[a] = product.astype(jnp.bfloat16).reshape(halves, half_rows, red)
        send_w(a, 0)
        return carry

    lax.fori_loop(0, box_count, weights, 0)

    for copy in rest:
        copy.wait()

    def local_terms(a, carry):
        w = own_w[a].reshape(skel, red)
        own = lax.dot_general(w, full_c[a], (((1,), (1,)), ((), ())), preferred_element_type=jnp.float32)
        cols = pl.ds(0, skel)
        near = base[a, :, :, cols].reshape(skel, skel).astype(jnp.float32)
        base[a, :, :, cols] = (near - own).astype(jnp.bfloat16).reshape(halves, half_rows, skel)
        for j in range(slots):
            cols = pl.ds((j + 1) * skel, skel)
            pair = jnp.dot(w, tile[table[0, a * slots + j]], preferred_element_type=jnp.float32)
            near = base[a, :, :, cols].reshape(skel, skel).astype(jnp.float32)
            base[a, :, :, cols] = (near - pair).astype(jnp.bfloat16).reshape(halves, half_rows, skel)
        return carry

    lax.fori_loop(0, box_count, local_terms, 0)

    for copy in list_copies:
        copy.wait()
    to_scalars = pltpu.make_async_copy(list_in, list_s, load_sem.at[first + 2 + halves])
    to_scalars.start()
    to_scalars.wait()

    def remote_terms(h):
        for d in range(2):
            pltpu.make_async_copy(wr[h].at[d], wr[h].at[d], w_recv.at[h, d]).wait()

        def one(k, carry):
            for d in range(2):
                pair = jnp.dot(
                    wr[h][d, list_s[d, 1, k]], tile[list_s[d, 0, k]], preferred_element_type=jnp.float32
                )
                rs[h][d, k] = pair.astype(jnp.bfloat16)
                pltpu.make_async_remote_copy(
                    src_ref=rs[h].at[d, k],
                    dst_ref=res[h].at[(1 - d) * FAR + k],
                    send_sem=r_send.at[h, d],
                    recv_sem=r_recv.at[h, 1 - d],
                    device_id=near_devices[d],
                    device_id_type=MESH,
                ).start()
            return carry

        lax.fori_loop(0, FAR, one, 0)

    def finish(h):
        for d in range(2):
            arrived = res[h].at[pl.ds(d * FAR, FAR)]
            pltpu.make_async_copy(arrived, arrived, r_recv.at[h, d]).wait()

        def one(a, carry):
            ob[h][:, a, :, pl.ds(0, skel)] = base[a, h, :, pl.ds(0, skel)].reshape(dests, 8, skel)
            for j in range(slots):
                cols = pl.ds((j + 1) * skel, skel)
                value = base[a, h, :, cols].astype(jnp.float32) - res[h][table[1, a * slots + j]].astype(jnp.float32)
                ob[h][:, a, :, cols] = value.reshape(dests, 8, skel).astype(jnp.bfloat16)
            return carry

        lax.fori_loop(0, box_count, one, 0)

    def spread(h):
        def slot(dx, dz, dc):
            to_x = lax.rem(x + dx, groups)
            to_z = lax.rem(z + h + 2 * dz, z_count)
            to_c = lax.rem(c + dc, 2)
            return (to_x * z_half + to_z // 2) * 2 + to_c, to_x * per_group + to_z * 2 + to_c

        def send(s, carry):
            place, to_b = slot(s % groups, (s // groups) % z_half, s // (groups * z_half))
            pltpu.make_async_remote_copy(
                src_ref=ob[h].at[place],
                dst_ref=stage.at[x, z // 2, lax.rem(z, 2), c],
                send_sem=st_send.at[h],
                recv_sem=st_recv.at[h, x],
                device_id=(to_b, g),
                device_id_type=MESH,
            ).start()
            return carry

        if h == 0:
            place, _ = slot(0, 0, 0)
            pltpu.make_async_copy(
                ob[h].at[place], stage.at[x, z // 2, lax.rem(z, 2), c], st_recv.at[h, x]
            ).start()
        lax.fori_loop(1 if h == 0 else 0, dests, send, 0)

    def forward(h):
        for step in (0, 1, 3, 2):
            from_x = lax.rem(x + step, groups)
            piece = stage.at[from_x, :, parity[h]]
            pltpu.make_async_copy(piece, piece, st_recv.at[h, from_x]).wait()
            place = out.at[:, parity[h], :, g]

            @pl.when(from_x == g)
            def _():
                pltpu.make_async_copy(piece, place, out_recv).start()

            @pl.when(from_x != g)
            def _():
                pltpu.make_async_remote_copy(
                    src_ref=piece,
                    dst_ref=place,
                    send_sem=out_send.at[h],
                    recv_sem=out_recv,
                    device_id=(b, from_x),
                    device_id_type=MESH,
                ).start()

    def send_w_half(h):
        def one(a, carry):
            send_w(a, h)
            return carry

        lax.fori_loop(0, box_count, one, 0)

    remote_terms(0)
    send_w_half(1)
    remote_terms(1)
    finish(0)
    spread(0)
    forward(0)
    finish(1)
    spread(1)
    forward(1)

    pltpu.make_async_copy(out, out, out_recv).wait()
    for h in range(halves):
        for d in range(2):
            pltpu.make_async_copy(wr[h].at[d], wr[h].at[d], w_send.at[h, d]).wait()
            pltpu.make_async_copy(rs[h].at[d], rs[h].at[d], r_send.at[h, d]).wait()
        sent = ob[h].at[pl.ds(0, dests - 1 if h == 0 else dests)]
        pltpu.make_async_copy(sent, sent, st_send.at[h]).wait()
        sent = stage.at[pl.ds(0, groups - 1), :, 0]
        pltpu.make_async_copy(sent, sent, out_send.at[h]).wait()


def per_device(groups, boxes_axis, coupling, inverse, tiles, near_block, neighbour, source_slot):
    box_count, skel, red = coupling.shape
    slots = neighbour.shape[1]
    total = box_count * slots
    width = near_block.shape[-1]
    rows = skel // boxes_axis
    half_rows = skel // HALVES
    z_half = boxes_axis // groups // 4
    device_now = lax.axis_index(("box", "grp"))
    lists, table = request_tables(neighbour, source_slot, device_now, boxes_axis * groups)
    half = jnp.bfloat16
    split = (box_count, groups, z_half, 2, 2 * rows)
    dests = boxes_axis // 2
    hbm = pl.BlockSpec(memory_space=pl.ANY)
    moved = pl.pallas_call(
        functools.partial(kernel, groups, boxes_axis),
        out_shape=jax.ShapeDtypeStruct((z_half, 2, 2, groups, box_count, rows, width), half),
        in_specs=[
            pl.BlockSpec(memory_space=pltpu.SMEM),
            pl.BlockSpec(memory_space=pltpu.VMEM),
            hbm, hbm, hbm, hbm, hbm,
        ],
        out_specs=hbm,
        scratch_shapes=[
            pltpu.VMEM((box_count, HALVES, half_rows, red), half),
            pltpu.VMEM((box_count, red, red), half),
            pltpu.VMEM((box_count, skel, red), half),
            pltpu.VMEM((total + 1, red, skel), half),
            pltpu.VMEM((box_count, HALVES, half_rows, width), half),
            pltpu.VMEM((box_count, HALVES, half_rows, red), half),
        ]
        + [pltpu.VMEM((2, box_count, half_rows, red), half)] * 2
        + [pltpu.VMEM((2, FAR, half_rows, skel), half)] * 2
        + [pltpu.VMEM((2 * FAR + 1, half_rows, skel), half)] * 2
        + [pltpu.VMEM((dests, box_count, rows, width), half)] * 2
        + [
            pltpu.VMEM((groups, z_half, 2, 2, box_count, rows, width), half),
            pltpu.VMEM(lists.shape, jnp.int32),
            pltpu.SMEM(lists.shape, jnp.int32),
            pltpu.SemaphoreType.DMA((3 * box_count + 3 + HALVES,)),
            pltpu.SemaphoreType.DMA((2,)),
            pltpu.SemaphoreType.DMA((2,)),
            pltpu.SemaphoreType.DMA((HALVES, 2)),
            pltpu.SemaphoreType.DMA((HALVES, 2)),
            pltpu.SemaphoreType.DMA((HALVES, 2)),
            pltpu.SemaphoreType.DMA((HALVES, 2)),
            pltpu.SemaphoreType.DMA((HALVES,)),
            pltpu.SemaphoreType.DMA((HALVES, groups)),
            pltpu.SemaphoreType.DMA((HALVES,)),
            pltpu.SemaphoreType.DMA,
        ],
        compiler_params=pltpu.CompilerParams(
            collective_id=0, has_side_effects=True, vmem_limit_bytes=56 * 2**20
        ),
        cost_estimate=pl.CostEstimate(flops=9 * 10**9, bytes_accessed=24 * 10**6, transcendentals=0),
    )(
        table,
        lists,
        coupling.reshape(split + (red,)),
        coupling,
        inverse,
        tiles.reshape(total, red, skel),
        near_block.reshape(split + (width,)),
    )
    return moved.reshape(-1, rows, width)


def solution(mesh):
    return jax.shard_map(
        functools.partial(per_device, mesh.shape["grp"], mesh.shape["box"]),
        mesh=mesh,
        in_specs=(
            P(("box", "grp"), None, None),
            P(("box", "grp"), None, None),
            P(("box", "grp"), None, None, None),
            P(("box", "grp"), None, None),
            P(("box", "grp"), None),
            P(("box", "grp"), None),
        ),
        out_specs=P("grp", "box", None),
        check_vma=False,
    )
```

```python
import functools

import jax
import jax.numpy as jnp
from jax import lax
from jax.experimental import pallas as pl
from jax.experimental.pallas import tpu as pltpu
from jax.sharding import PartitionSpec as P

FAR = 12
GROUP = 3
MESH = pl.DeviceIdType.MESH


def request_tables(neighbour, source_slot, device_now, device_count):
    box_count, slot_count = neighbour.shape
    total = box_count * slot_count
    order = jnp.arange(total, dtype=jnp.int32)
    spot = (jnp.arange(box_count)[:, None] * slot_count + jnp.arange(slot_count)[None, :]).astype(jnp.int32)
    picks = (spot[None] == order[:, None, None]).astype(jnp.int32)
    flat = jnp.sum(picks * (neighbour * slot_count + source_slot)[None], axis=(1, 2))
    owner = flat // total
    place = flat - owner * total
    asked = jnp.stack(
        [
            owner == (device_now + 1) % device_count,
            owner == (device_now + device_count - 1) % device_count,
        ]
    )
    before = (order[None, :] < order[:, None]).astype(jnp.int32)
    rank = jnp.sum(before[None] * asked[:, None, :].astype(jnp.int32), axis=2)
    lanes = jnp.arange(128, dtype=jnp.int32)
    onehot = jnp.logical_and(
        jnp.logical_and(rank[:, None, :] == lanes[None, :, None], lanes[None, :, None] < FAR), asked[:, None, :]
    ).astype(jnp.int32)
    tile_list = jnp.sum(onehot * place[None, None, :], axis=2)
    box_list = jnp.sum(onehot * (order // slot_count)[None, None, :], axis=2)
    here = jnp.logical_not(jnp.logical_or(asked[0], asked[1]))
    local_tile = jnp.where(here, place, total)
    result_at = jnp.where(asked[0], rank[0], jnp.where(asked[1], FAR + rank[1], 2 * FAR))
    own = jnp.pad(jnp.stack([local_tile, result_at]), ((0, 0), (0, 128 - total)))
    rows = jnp.stack([jnp.stack([tile_list[0], box_list[0]]), jnp.stack([tile_list[1], box_list[1]]), own])
    return jnp.pad(rows, ((0, 0), (0, 6), (0, 0)))


def kernel(
    groups, boxes_axis, chunks, slots,
    lists, split_coupling, coupling, inverse, tiles, split_near,
    out,
    cp, inv, full_c, tile, base, own_w, stage, list_in, list_s,
    load_sem, c_sem, near_sem, list_send, list_recv, w_send, w_recv, r_send, r_recv,
    st_send, st_recv, out_send, out_recv, *buffers,
):
    box_count, skel, red = cp.shape
    total = box_count * slots
    per_group = boxes_axis // groups
    z_count = chunks
    piece_rows = 16
    chunk_rows = groups * piece_rows
    dests = groups * 2
    wr, rs, res, ob = (buffers[n * chunks : (n + 1) * chunks] for n in range(4))
    b = lax.axis_index("box")
    g = lax.axis_index("grp")
    x = b // per_group
    z = (b % per_group) // 2
    c = b % 2
    count = boxes_axis * groups
    here = b * groups + g
    after = lax.rem(here + 1, count)
    behind = lax.rem(here + count - 1, count)
    beside = ((after // groups, after % groups), (behind // groups, behind % groups))

    def to_xz(q, dx):
        return lax.rem(x + dx, groups), lax.rem(z + q - dx + 2 * z_count, z_count)

    def load_c(q, dx):
        to_x, to_z = to_xz(q, dx)
        rows = pl.ds((q * groups + dx) * piece_rows, piece_rows)
        return pltpu.make_async_copy(split_coupling.at[:, to_x, to_z], cp.at[:, rows], c_sem.at[q * groups + dx])

    def load_near(q, dx):
        to_x, to_z = to_xz(q, dx)
        rows = pl.ds(dx * piece_rows, piece_rows)
        return pltpu.make_async_copy(
            split_near.at[:, to_x, to_z], base.at[q, :, rows], near_sem.at[q * groups + dx]
        )

    def load_inv(a):
        return pltpu.make_async_copy(inverse.at[a], inv.at[a], load_sem.at[a])

    pieces = [(q, dx) for q in range(chunks) for dx in range(groups)]
    for q, dx in pieces:
        load_c(q, dx).start()
    for a in range(box_count):
        load_inv(a).start()
    barrier = pltpu.get_barrier_semaphore()

    def greet(k, carry):
        pl.semaphore_signal(barrier, inc=1, device_id=(lax.rem(b + k, boxes_axis), g), device_id_type=MESH)
        return carry

    lax.fori_loop(1, boxes_axis, greet, 0)
    for k in range(1, groups):
        pl.semaphore_signal(barrier, inc=1, device_id=(b, lax.rem(g + k, groups)), device_id_type=MESH)
    for device in beside:
        pl.semaphore_signal(barrier, inc=1, device_id=device, device_id_type=MESH)

    load_tiles = pltpu.make_async_copy(tiles, tile.at[pl.ds(0, total)], load_sem.at[box_count])
    load_full = pltpu.make_async_copy(coupling, full_c, load_sem.at[box_count + 1])
    load_own = pltpu.make_async_copy(lists.at[2], list_s.at[2], load_sem.at[box_count + 2])
    load_full.start()
    load_tiles.start()
    for q, dx in pieces:
        load_near(q, dx).start()
    load_own.start()
    tile[total] = jnp.zeros_like(tile[total])
    for q in range(chunks):
        res[q][2 * FAR] = jnp.zeros_like(res[q][2 * FAR])

    def send_w(q, a):
        for d in range(2):
            pltpu.make_async_remote_copy(
                src_ref=own_w.at[q, a],
                dst_ref=wr[q].at[1 - d, a],
                send_sem=w_send.at[q, d],
                recv_sem=w_recv.at[q, 1 - d],
                device_id=beside[d],
                device_id_type=MESH,
            ).start()

    def send_w_all(q):
        def one(a, carry):
            send_w(q, a)
            return carry

        lax.fori_loop(0, box_count, one, 0)

    for q, dx in pieces:
        load_c(q, dx).wait()

    def weights(a, carry):
        load_inv(a).wait()
        product = jnp.dot(cp[a], inv[a], preferred_element_type=jnp.float32)
        own_w[:, a] = product.astype(jnp.bfloat16).reshape(chunks, chunk_rows, red)
        return carry

    lax.fori_loop(0, 1, weights, 0)
    pl.semaphore_wait(barrier, boxes_axis - 1 + groups - 1 + 2)

    def weights_sent(a, carry):
        send_w(0, a)

        @pl.when(a + 1 < box_count)
        def _():
            weights(a + 1, 0)

        return carry

    lax.fori_loop(0, box_count, weights_sent, 0)
    send_w_all(1)
    list_copies = [
        pltpu.make_async_remote_copy(
            src_ref=lists.at[d],
            dst_ref=list_in.at[1 - d],
            send_sem=list_send.at[d],
            recv_sem=list_recv.at[1 - d],
            device_id=beside[d],
            device_id_type=MESH,
        )
        for d in range(2)
    ]
    for copy in list_copies:
        copy.start()


    load_full.wait()
    load_tiles.wait()
    for q, dx in pieces:
        load_near(q, dx).wait()
    load_own.wait()

    def local_terms(a, carry):
        w = own_w[:, a].reshape(skel, red)
        own = lax.dot_general(w, full_c[a], (((1,), (1,)), ((), ())), preferred_element_type=jnp.float32)
        cols = pl.ds(0, skel)
        near = base[:, a, :, cols].reshape(skel, skel).astype(jnp.float32)
        base[:, a, :, cols] = (near - own).astype(jnp.bfloat16).reshape(chunks, chunk_rows, skel)
        for j in range(slots):
            cols = pl.ds((j + 1) * skel, skel)
            pair = jnp.dot(w, tile[list_s[2, 0, a * slots + j]], preferred_element_type=jnp.float32)
            near = base[:, a, :, cols].reshape(skel, skel).astype(jnp.float32)
            base[:, a, :, cols] = (near - pair).astype(jnp.bfloat16).reshape(chunks, chunk_rows, skel)
        return carry

    lax.fori_loop(0, box_count, local_terms, 0)

    for copy in list_copies:
        copy.wait()
    to_scalars = pltpu.make_async_copy(list_in, list_s.at[pl.ds(0, 2)], load_sem.at[box_count + 3])
    to_scalars.start()
    to_scalars.wait()

    def remote_terms(q):
        for d in range(2):
            pltpu.make_async_copy(wr[q].at[d], wr[q].at[d], w_recv.at[q, d]).wait()

        def one(n, carry):
            for d in range(2):
                for i in range(GROUP):
                    k = n * GROUP + i
                    pair = jnp.dot(
                        wr[q][d, list_s[d, 1, k]], tile[list_s[d, 0, k]], preferred_element_type=jnp.float32
                    )
                    rs[q][d, k] = pair.astype(jnp.bfloat16)
                pltpu.make_async_remote_copy(
                    src_ref=rs[q].at[d, pl.ds(n * GROUP, GROUP)],
                    dst_ref=res[q].at[pl.ds((1 - d) * FAR + n * GROUP, GROUP)],
                    send_sem=r_send.at[q, d],
                    recv_sem=r_recv.at[q, 1 - d],
                    device_id=beside[d],
                    device_id_type=MESH,
                ).start()
            return carry

        lax.fori_loop(0, FAR // GROUP, one, 0)

    def finish(q):
        for d in range(2):
            arrived = res[q].at[pl.ds(d * FAR, FAR)]
            pltpu.make_async_copy(arrived, arrived, r_recv.at[q, d]).wait()

        def one(a, carry):
            ob[q][:, a, :, pl.ds(0, skel)] = base[q, a, :, pl.ds(0, skel)].reshape(dests, 8, skel)
            for j in range(slots):
                cols = pl.ds((j + 1) * skel, skel)
                value = base[q, a, :, cols].astype(jnp.float32) - res[q][list_s[2, 1, a * slots + j]].astype(jnp.float32)
                ob[q][:, a, :, cols] = value.reshape(dests, 8, skel).astype(jnp.bfloat16)
            return carry

        lax.fori_loop(0, box_count, one, 0)

        def send(s, carry):
            dx, to_c = s % groups, lax.rem(c + s // groups, 2)
            to_x, to_z = to_xz(q, dx)
            pltpu.make_async_remote_copy(
                src_ref=ob[q].at[dx * 2 + to_c],
                dst_ref=stage.at[x, z, c],
                send_sem=st_send.at[q],
                recv_sem=st_recv.at[q, x],
                device_id=(to_x * per_group + to_z * 2 + to_c, g),
                device_id_type=MESH,
            ).start()
            return carry

        if q == 0:
            pltpu.make_async_copy(ob[q].at[c], stage.at[x, z, c], st_recv.at[q, x]).start()
        lax.fori_loop(1 if q == 0 else 0, dests, send, 0)

    def forward(q):
        for step in (0, 1, 3, 2):
            from_x = lax.rem(x + step, groups)
            from_z = lax.rem(z - q + lax.rem(groups - step, groups) + 2 * z_count, z_count)
            piece = stage.at[from_x, from_z]
            pltpu.make_async_copy(piece, piece, st_recv.at[q, from_x]).wait()
            place = out.at[from_z, :, g]

            @pl.when(from_x == g)
            def _():
                pltpu.make_async_copy(piece, place, out_recv).start()

            @pl.when(from_x != g)
            def _():
                pltpu.make_async_remote_copy(
                    src_ref=piece,
                    dst_ref=place,
                    send_sem=out_send.at[q],
                    recv_sem=out_recv,
                    device_id=(b, from_x),
                    device_id_type=MESH,
                ).start()

    plan = PLAN
    steps = {"t": remote_terms, "w": send_w_all, "f": finish, "o": forward}
    for step in plan.split():
        steps[step[0]](int(step[1:]))

    pltpu.make_async_copy(out, out, out_recv).wait()
    for q in range(chunks):
        for d in range(2):
            pltpu.make_async_copy(wr[q].at[d], wr[q].at[d], w_send.at[q, d]).wait()
            pltpu.make_async_copy(rs[q].at[d], rs[q].at[d], r_send.at[q, d]).wait()
        sent = ob[q].at[pl.ds(0, dests - 1 if q == 0 else dests)]
        pltpu.make_async_copy(sent, sent, st_send.at[q]).wait()
        sent = stage.at[pl.ds(0, groups - 1), 0]
        pltpu.make_async_copy(sent, sent, out_send.at[q]).wait()


PLAN = "t0 w2 t1 w3 f0 t2 f1 o0 t3 f2 o1 f3 o2 o3"


def per_device(groups, boxes_axis, coupling, inverse, tiles, near_block, neighbour, source_slot):
    box_count, skel, red = coupling.shape
    slots = neighbour.shape[1]
    total = box_count * slots
    width = near_block.shape[-1]
    rows = skel // boxes_axis
    chunks = boxes_axis // groups // 2
    chunk_rows = skel // chunks
    device_now = lax.axis_index(("box", "grp"))
    lists = request_tables(neighbour, source_slot, device_now, boxes_axis * groups)
    half = jnp.bfloat16
    split = (box_count, groups, chunks, 2 * rows)
    hbm = pl.BlockSpec(memory_space=pltpu.HBM)
    moved = pl.pallas_call(
        functools.partial(kernel, groups, boxes_axis, chunks, slots),
        out_shape=jax.ShapeDtypeStruct((chunks, 2, groups, box_count, rows, width), half),
        in_specs=[pl.BlockSpec(memory_space=pltpu.VMEM), hbm, hbm, hbm, hbm, hbm],
        out_specs=pl.BlockSpec(memory_space=pl.ANY),
        scratch_shapes=[
            pltpu.VMEM((box_count, skel, red), half),
            pltpu.VMEM((box_count, red, red), half),
            pltpu.VMEM((box_count, skel, red), half),
            pltpu.VMEM((total + 1, red, skel), half),
            pltpu.VMEM((chunks, box_count, chunk_rows, width), half),
            pltpu.VMEM((chunks, box_count, chunk_rows, red), half),
            pltpu.VMEM((groups, chunks, 2, box_count, rows, width), half),
            pltpu.VMEM((2,) + lists.shape[1:], jnp.int32),
            pltpu.SMEM(lists.shape, jnp.int32),
            pltpu.SemaphoreType.DMA((box_count + 4,)),
            pltpu.SemaphoreType.DMA((chunks * groups,)),
            pltpu.SemaphoreType.DMA((chunks * groups,)),
            pltpu.SemaphoreType.DMA((2,)),
            pltpu.SemaphoreType.DMA((2,)),
            pltpu.SemaphoreType.DMA((chunks, 2)),
            pltpu.SemaphoreType.DMA((chunks, 2)),
            pltpu.SemaphoreType.DMA((chunks, 2)),
            pltpu.SemaphoreType.DMA((chunks, 2)),
            pltpu.SemaphoreType.DMA((chunks,)),
            pltpu.SemaphoreType.DMA((chunks, groups)),
            pltpu.SemaphoreType.DMA((chunks,)),
            pltpu.SemaphoreType.DMA,
        ]
        + [pltpu.VMEM((2, box_count, chunk_rows, red), half)] * chunks
        + [pltpu.VMEM((2, FAR, chunk_rows, skel), half)] * chunks
        + [pltpu.VMEM((2 * FAR + 1, chunk_rows, skel), half)] * chunks
        + [pltpu.VMEM((2 * groups, box_count, rows, width), half)] * chunks,
        compiler_params=pltpu.CompilerParams(
            collective_id=0, has_side_effects=True, vmem_limit_bytes=46 * 2**20
        ),
        cost_estimate=pl.CostEstimate(flops=9 * 10**9, bytes_accessed=24 * 10**6, transcendentals=0),
    )(
        lists,
        coupling.reshape(split + (red,)),
        coupling,
        inverse,
        tiles.reshape(total, red, skel),
        near_block.reshape(split + (width,)),
    )
    return moved.reshape(-1, rows, width)


def solution(mesh):
    return jax.shard_map(
        functools.partial(per_device, mesh.shape["grp"], mesh.shape["box"]),
        mesh=mesh,
        in_specs=(
            P(("box", "grp"), None, None),
            P(("box", "grp"), None, None),
            P(("box", "grp"), None, None, None),
            P(("box", "grp"), None, None),
            P(("box", "grp"), None),
            P(("box", "grp"), None),
        ),
        out_specs=P("grp", "box", None),
        check_vma=False,
    )
```

```python
import functools

import jax
import jax.numpy as jnp
from jax import lax
from jax.experimental import pallas as pl
from jax.experimental.pallas import tpu as pltpu
from jax.sharding import PartitionSpec as P

FAR = 12
GROUP = 3
MESH = pl.DeviceIdType.MESH


def request_tables(neighbour, source_slot, device_now, device_count):
    box_count, slot_count = neighbour.shape
    total = box_count * slot_count
    order = jnp.arange(total, dtype=jnp.int32)
    spot = (jnp.arange(box_count)[:, None] * slot_count + jnp.arange(slot_count)[None, :]).astype(jnp.int32)
    picks = (spot[None] == order[:, None, None]).astype(jnp.int32)
    flat = jnp.sum(picks * (neighbour * slot_count + source_slot)[None], axis=(1, 2))
    owner = flat // total
    place = flat - owner * total
    asked = jnp.stack(
        [
            owner == (device_now + 1) % device_count,
            owner == (device_now + device_count - 1) % device_count,
        ]
    )
    before = (order[None, :] < order[:, None]).astype(jnp.int32)
    rank = jnp.sum(before[None] * asked[:, None, :].astype(jnp.int32), axis=2)
    lanes = jnp.arange(128, dtype=jnp.int32)
    onehot = jnp.logical_and(
        jnp.logical_and(rank[:, None, :] == lanes[None, :, None], lanes[None, :, None] < FAR), asked[:, None, :]
    ).astype(jnp.int32)
    tile_list = jnp.sum(onehot * place[None, None, :], axis=2)
    box_list = jnp.sum(onehot * (order // slot_count)[None, None, :], axis=2)
    here = jnp.logical_not(jnp.logical_or(asked[0], asked[1]))
    local_tile = jnp.where(here, place, total)
    result_at = jnp.where(asked[0], rank[0], jnp.where(asked[1], FAR + rank[1], 2 * FAR))
    own = jnp.pad(jnp.stack([local_tile, result_at]), ((0, 0), (0, 128 - total)))
    rows = jnp.stack([jnp.stack([tile_list[0], box_list[0]]), jnp.stack([tile_list[1], box_list[1]]), own])
    return jnp.pad(rows, ((0, 0), (0, 6), (0, 0)))


def kernel(
    groups, boxes_axis, chunks, slots,
    lists, split_coupling, coupling, inverse, tiles, split_near,
    out,
    cp, inv, full_c, tile, base, own_w, stage, list_in, list_s,
    load_sem, c_sem, near_sem, list_send, list_recv, w_send, w_recv, r_send, r_recv,
    st_send, st_recv, out_send, out_recv, *buffers,
):
    box_count, skel, red = cp.shape
    total = box_count * slots
    per_group = boxes_axis // groups
    z_count = chunks
    piece_rows = 16
    chunk_rows = groups * piece_rows
    dests = groups * 2
    wr, rs, res, ob = (buffers[n * chunks : (n + 1) * chunks] for n in range(4))
    b = lax.axis_index("box")
    g = lax.axis_index("grp")
    x = b // per_group
    z = (b % per_group) // 2
    c = b % 2
    count = boxes_axis * groups
    here = b * groups + g
    after = lax.rem(here + 1, count)
    behind = lax.rem(here + count - 1, count)
    beside = ((after // groups, after % groups), (behind // groups, behind % groups))

    def to_xz(q, dx):
        return lax.rem(x + dx, groups), lax.rem(z + q - dx + 2 * z_count, z_count)

    def load_c(q, dx):
        to_x, to_z = to_xz(q, dx)
        rows = pl.ds((q * groups + dx) * piece_rows, piece_rows)
        return pltpu.make_async_copy(split_coupling.at[:, to_x, to_z], cp.at[:, rows], c_sem.at[q * groups + dx])

    def load_near(q, dx):
        to_x, to_z = to_xz(q, dx)
        rows = pl.ds(dx * piece_rows, piece_rows)
        return pltpu.make_async_copy(
            split_near.at[:, to_x, to_z], base.at[q, :, rows], near_sem.at[q * groups + dx]
        )

    def load_inv(a):
        return pltpu.make_async_copy(inverse.at[a], inv.at[a], load_sem.at[a])

    pieces = [(q, dx) for q in range(chunks) for dx in range(groups)]
    for q, dx in pieces:
        load_c(q, dx).start()
    for a in range(box_count):
        load_inv(a).start()
    barrier = pltpu.get_barrier_semaphore()

    def greet(k, carry):
        pl.semaphore_signal(barrier, inc=1, device_id=(lax.rem(b + k, boxes_axis), g), device_id_type=MESH)
        return carry

    lax.fori_loop(1, boxes_axis, greet, 0)
    for k in range(1, groups):
        pl.semaphore_signal(barrier, inc=1, device_id=(b, lax.rem(g + k, groups)), device_id_type=MESH)
    for device in beside:
        pl.semaphore_signal(barrier, inc=1, device_id=device, device_id_type=MESH)

    load_tiles = pltpu.make_async_copy(tiles, tile.at[pl.ds(0, total)], load_sem.at[box_count])
    load_full = pltpu.make_async_copy(coupling, full_c, load_sem.at[box_count + 1])
    load_own = pltpu.make_async_copy(lists.at[2], list_s.at[2], load_sem.at[box_count + 2])
    load_full.start()
    load_tiles.start()
    for q, dx in pieces:
        load_near(q, dx).start()
    load_own.start()
    tile[total] = jnp.zeros_like(tile[total])
    for q in range(chunks):
        res[q][2 * FAR] = jnp.zeros_like(res[q][2 * FAR])

    def send_w(q, a):
        for d in range(2):
            pltpu.make_async_remote_copy(
                src_ref=own_w.at[q, a],
                dst_ref=wr[q].at[1 - d, a],
                send_sem=w_send.at[q, d],
                recv_sem=w_recv.at[q, 1 - d],
                device_id=beside[d],
                device_id_type=MESH,
            ).start()

    def send_w_all(q):
        def one(a, carry):
            send_w(q, a)
            return carry

        lax.fori_loop(0, box_count, one, 0)

    for q, dx in pieces:
        load_c(q, dx).wait()

    def weights(a, carry):
        load_inv(a).wait()
        product = jnp.dot(cp[a], inv[a], preferred_element_type=jnp.float32)
        own_w[:, a] = product.astype(jnp.bfloat16).reshape(chunks, chunk_rows, red)
        return carry

    lax.fori_loop(0, 1, weights, 0)
    pl.semaphore_wait(barrier, boxes_axis - 1 + groups - 1 + 2)

    def weights_sent(a, carry):
        send_w(0, a)

        @pl.when(a + 1 < box_count)
        def _():
            weights(a + 1, 0)

        return carry

    lax.fori_loop(0, box_count, weights_sent, 0)
    list_copies = [
        pltpu.make_async_remote_copy(
            src_ref=lists.at[d],
            dst_ref=list_in.at[1 - d],
            send_sem=list_send.at[d],
            recv_sem=list_recv.at[1 - d],
            device_id=beside[d],
            device_id_type=MESH,
        )
        for d in range(2)
    ]
    for copy in list_copies:
        copy.start()


    load_full.wait()
    load_tiles.wait()
    for q, dx in pieces:
        load_near(q, dx).wait()
    load_own.wait()

    def local_terms(a, carry):
        w = own_w[:, a].reshape(skel, red)
        own = lax.dot_general(w, full_c[a], (((1,), (1,)), ((), ())), preferred_element_type=jnp.float32)
        cols = pl.ds(0, skel)
        near = base[:, a, :, cols].reshape(skel, skel).astype(jnp.float32)
        base[:, a, :, cols] = (near - own).astype(jnp.bfloat16).reshape(chunks, chunk_rows, skel)
        for j in range(slots):
            cols = pl.ds((j + 1) * skel, skel)
            pair = jnp.dot(w, tile[list_s[2, 0, a * slots + j]], preferred_element_type=jnp.float32)
            near = base[:, a, :, cols].reshape(skel, skel).astype(jnp.float32)
            base[:, a, :, cols] = (near - pair).astype(jnp.bfloat16).reshape(chunks, chunk_rows, skel)
        return carry

    lax.fori_loop(0, box_count, local_terms, 0)
    send_w_all(1)

    for copy in list_copies:
        copy.wait()
    to_scalars = pltpu.make_async_copy(list_in, list_s.at[pl.ds(0, 2)], load_sem.at[box_count + 3])
    to_scalars.start()
    to_scalars.wait()

    def remote_terms(q):
        for d in range(2):
            pltpu.make_async_copy(wr[q].at[d], wr[q].at[d], w_recv.at[q, d]).wait()

        def one(n, carry):
            for d in range(2):
                for i in range(GROUP):
                    k = n * GROUP + i
                    pair = jnp.dot(
                        wr[q][d, list_s[d, 1, k]], tile[list_s[d, 0, k]], preferred_element_type=jnp.float32
                    )
                    rs[q][d, k] = pair.astype(jnp.bfloat16)
                pltpu.make_async_remote_copy(
                    src_ref=rs[q].at[d, pl.ds(n * GROUP, GROUP)],
                    dst_ref=res[q].at[pl.ds((1 - d) * FAR + n * GROUP, GROUP)],
                    send_sem=r_send.at[q, d],
                    recv_sem=r_recv.at[q, 1 - d],
                    device_id=beside[d],
                    device_id_type=MESH,
                ).start()
            return carry

        lax.fori_loop(0, FAR // GROUP, one, 0)

    def finish(q):
        for d in range(2):
            arrived = res[q].at[pl.ds(d * FAR, FAR)]
            pltpu.make_async_copy(arrived, arrived, r_recv.at[q, d]).wait()

        def one(a, carry):
            ob[q][:, a, :, pl.ds(0, skel)] = base[q, a, :, pl.ds(0, skel)].reshape(dests, 8, skel)
            for j in range(slots):
                cols = pl.ds((j + 1) * skel, skel)
                value = base[q, a, :, cols].astype(jnp.float32) - res[q][list_s[2, 1, a * slots + j]].astype(jnp.float32)
                ob[q][:, a, :, cols] = value.reshape(dests, 8, skel).astype(jnp.bfloat16)
            return carry

        lax.fori_loop(0, box_count, one, 0)

        def send(s, carry):
            dx, to_c = s % groups, lax.rem(c + s // groups, 2)
            to_x, to_z = to_xz(q, dx)
            pltpu.make_async_remote_copy(
                src_ref=ob[q].at[dx * 2 + to_c],
                dst_ref=stage.at[x, z, c],
                send_sem=st_send.at[q],
                recv_sem=st_recv.at[q, x],
                device_id=(to_x * per_group + to_z * 2 + to_c, g),
                device_id_type=MESH,
            ).start()
            return carry

        if q == 0:
            pltpu.make_async_copy(ob[q].at[c], stage.at[x, z, c], st_recv.at[q, x]).start()
        lax.fori_loop(1 if q == 0 else 0, dests, send, 0)

    def forward(q):
        for step in (0, 1, 3, 2):
            from_x = lax.rem(x + step, groups)
            from_z = lax.rem(z - q + lax.rem(groups - step, groups) + 2 * z_count, z_count)
            piece = stage.at[from_x, from_z]
            pltpu.make_async_copy(piece, piece, st_recv.at[q, from_x]).wait()
            place = out.at[from_z, :, g]

            @pl.when(from_x == g)
            def _():
                pltpu.make_async_copy(piece, place, out_recv).start()

            @pl.when(from_x != g)
            def _():
                pltpu.make_async_remote_copy(
                    src_ref=piece,
                    dst_ref=place,
                    send_sem=out_send.at[q],
                    recv_sem=out_recv,
                    device_id=(b, from_x),
                    device_id_type=MESH,
                ).start()

    for step, q in (
        (remote_terms, 0), (send_w_all, 2), (remote_terms, 1), (send_w_all, 3), (finish, 0), (remote_terms, 2),
        (finish, 1), (forward, 0), (remote_terms, 3), (finish, 2), (forward, 1), (finish, 3), (forward, 2), (forward, 3),
    ):
        step(q)

    pltpu.make_async_copy(out, out, out_recv).wait()
    for q in range(chunks):
        for d in range(2):
            pltpu.make_async_copy(wr[q].at[d], wr[q].at[d], w_send.at[q, d]).wait()
            pltpu.make_async_copy(rs[q].at[d], rs[q].at[d], r_send.at[q, d]).wait()
        sent = ob[q].at[pl.ds(0, dests - 1 if q == 0 else dests)]
        pltpu.make_async_copy(sent, sent, st_send.at[q]).wait()
        sent = stage.at[pl.ds(0, groups - 1), 0]
        pltpu.make_async_copy(sent, sent, out_send.at[q]).wait()


def per_device(groups, boxes_axis, coupling, inverse, tiles, near_block, neighbour, source_slot):
    box_count, skel, red = coupling.shape
    slots = neighbour.shape[1]
    total = box_count * slots
    width = near_block.shape[-1]
    rows = skel // boxes_axis
    chunks = boxes_axis // groups // 2
    chunk_rows = skel // chunks
    device_now = lax.axis_index(("box", "grp"))
    lists = request_tables(neighbour, source_slot, device_now, boxes_axis * groups)
    half = jnp.bfloat16
    split = (box_count, groups, chunks, 2 * rows)
    hbm = pl.BlockSpec(memory_space=pl.ANY)
    big = (coupling.reshape(split + (red,)), coupling, inverse, tiles.reshape(total, red, skel), near_block.reshape(split + (width,)))
    big = [pltpu.with_memory_space_constraint(array, pltpu.HBM) for array in big]
    moved = pl.pallas_call(
        functools.partial(kernel, groups, boxes_axis, chunks, slots),
        out_shape=pltpu.VMEM((chunks, 2, groups, box_count, rows, width), half),
        in_specs=[pl.BlockSpec(memory_space=pltpu.VMEM), hbm, hbm, hbm, hbm, hbm],
        out_specs=pl.BlockSpec(memory_space=pl.ANY),
        scratch_shapes=[
            pltpu.VMEM((box_count, skel, red), half),
            pltpu.VMEM((box_count, red, red), half),
            pltpu.VMEM((box_count, skel, red), half),
            pltpu.VMEM((total + 1, red, skel), half),
            pltpu.VMEM((chunks, box_count, chunk_rows, width), half),
            pltpu.VMEM((chunks, box_count, chunk_rows, red), half),
            pltpu.VMEM((groups, chunks, 2, box_count, rows, width), half),
            pltpu.VMEM((2,) + lists.shape[1:], jnp.int32),
            pltpu.SMEM(lists.shape, jnp.int32),
            pltpu.SemaphoreType.DMA((box_count + 4,)),
            pltpu.SemaphoreType.DMA((chunks * groups,)),
            pltpu.SemaphoreType.DMA((chunks * groups,)),
            pltpu.SemaphoreType.DMA((2,)),
            pltpu.SemaphoreType.DMA((2,)),
            pltpu.SemaphoreType.DMA((chunks, 2)),
            pltpu.SemaphoreType.DMA((chunks, 2)),
            pltpu.SemaphoreType.DMA((chunks, 2)),
            pltpu.SemaphoreType.DMA((chunks, 2)),
            pltpu.SemaphoreType.DMA((chunks,)),
            pltpu.SemaphoreType.DMA((chunks, groups)),
            pltpu.SemaphoreType.DMA((chunks,)),
            pltpu.SemaphoreType.DMA,
        ]
        + [pltpu.VMEM((2, box_count, chunk_rows, red), half)] * chunks
        + [pltpu.VMEM((2, FAR, chunk_rows, skel), half)] * chunks
        + [pltpu.VMEM((2 * FAR + 1, chunk_rows, skel), half)] * chunks
        + [pltpu.VMEM((2 * groups, box_count, rows, width), half)] * chunks,
        compiler_params=pltpu.CompilerParams(
            collective_id=0, has_side_effects=True, vmem_limit_bytes=48 * 2**20
        ),
        cost_estimate=pl.CostEstimate(flops=9 * 10**9, bytes_accessed=24 * 10**6, transcendentals=0),
    )(
        lists,
        *big,
    )
    return moved.reshape(-1, rows, width)


def solution(mesh):
    return jax.shard_map(
        functools.partial(per_device, mesh.shape["grp"], mesh.shape["box"]),
        mesh=mesh,
        in_specs=(
            P(("box", "grp"), None, None),
            P(("box", "grp"), None, None),
            P(("box", "grp"), None, None, None),
            P(("box", "grp"), None, None),
            P(("box", "grp"), None),
            P(("box", "grp"), None),
        ),
        out_specs=P("grp", "box", None),
        check_vma=False,
    )
```

```python
import functools

import jax
import jax.numpy as jnp
from jax import lax
from jax.experimental import pallas as pl
from jax.experimental.pallas import tpu as pltpu
from jax.sharding import PartitionSpec as P

FAR = 12
GROUP = 3
MESH = pl.DeviceIdType.MESH


def kernel(
    groups, boxes_axis, chunks, slots,
    neighbour, source_slot, split_coupling, coupling, inverse, tiles, split_near,
    out,
    cp, inv, full_c, tile, base, own_w, stage, list_out, list_in, list_s, asked_s, place_s, near_s, slot_s,
    load_sem, c_sem, near_sem, list_send, list_recv, w_send, w_recv, r_send, r_recv,
    st_send, st_recv, out_send, out_recv, *buffers,
):
    box_count, skel, red = cp.shape
    total = box_count * slots
    per_group = boxes_axis // groups
    z_count = chunks
    piece_rows = 16
    chunk_rows = groups * piece_rows
    dests = groups * 2
    wr, rs, res, ob = (buffers[n * chunks : (n + 1) * chunks] for n in range(4))
    b = lax.axis_index("box")
    g = lax.axis_index("grp")
    x = b // per_group
    z = (b % per_group) // 2
    c = b % 2
    count = boxes_axis * groups
    here = b * groups + g
    after = lax.rem(here + 1, count)
    behind = lax.rem(here + count - 1, count)
    beside = ((after // groups, after % groups), (behind // groups, behind % groups))

    def to_xz(q, dx):
        return lax.rem(x + dx, groups), lax.rem(z + q - dx + 2 * z_count, z_count)

    def load_c(q, dx):
        to_x, to_z = to_xz(q, dx)
        rows = pl.ds((q * groups + dx) * piece_rows, piece_rows)
        return pltpu.make_async_copy(split_coupling.at[:, to_x, to_z], cp.at[:, rows], c_sem.at[q * groups + dx])

    def load_near(q, dx):
        to_x, to_z = to_xz(q, dx)
        rows = pl.ds(dx * piece_rows, piece_rows)
        return pltpu.make_async_copy(
            split_near.at[:, to_x, to_z], base.at[q, :, rows], near_sem.at[q * groups + dx]
        )

    def load_inv(a):
        return pltpu.make_async_copy(inverse.at[a], inv.at[a], load_sem.at[a])

    pieces = [(q, dx) for q in range(chunks) for dx in range(groups)]
    for q, dx in pieces:
        load_c(q, dx).start()
    for a in range(box_count):
        load_inv(a).start()
    barrier = pltpu.get_barrier_semaphore()

    def greet(k, carry):
        pl.semaphore_signal(barrier, inc=1, device_id=(lax.rem(b + k, boxes_axis), g), device_id_type=MESH)
        return carry

    lax.fori_loop(1, boxes_axis, greet, 0)
    for k in range(1, groups):
        pl.semaphore_signal(barrier, inc=1, device_id=(b, lax.rem(g + k, groups)), device_id_type=MESH)
    for device in beside:
        pl.semaphore_signal(barrier, inc=1, device_id=device, device_id_type=MESH)

    load_tiles = pltpu.make_async_copy(tiles, tile.at[pl.ds(0, total)], load_sem.at[box_count])
    load_full = pltpu.make_async_copy(coupling, full_c, load_sem.at[box_count + 1])
    load_own = [
        pltpu.make_async_copy(neighbour, near_s, load_sem.at[box_count + 2]),
        pltpu.make_async_copy(source_slot, slot_s, load_sem.at[box_count + 4]),
    ]
    load_full.start()
    load_tiles.start()
    for q, dx in pieces:
        load_near(q, dx).start()
    for copy in load_own:
        copy.start()
    tile[total] = jnp.zeros_like(tile[total])
    for q in range(chunks):
        res[q][2 * FAR] = jnp.zeros_like(res[q][2 * FAR])

    def send_w(q, a):
        for d in range(2):
            pltpu.make_async_remote_copy(
                src_ref=own_w.at[q, a],
                dst_ref=wr[q].at[1 - d, a],
                send_sem=w_send.at[q, d],
                recv_sem=w_recv.at[q, 1 - d],
                device_id=beside[d],
                device_id_type=MESH,
            ).start()

    def send_w_all(q):
        for d in range(2):
            pltpu.make_async_remote_copy(
                src_ref=own_w.at[q],
                dst_ref=wr[q].at[1 - d],
                send_sem=w_send.at[q, d],
                recv_sem=w_recv.at[q, 1 - d],
                device_id=beside[d],
                device_id_type=MESH,
            ).start()

    for q, dx in pieces:
        load_c(q, dx).wait()

    def weights(a, carry):
        load_inv(a).wait()
        product = jnp.dot(cp[a], inv[a], preferred_element_type=jnp.float32)
        own_w[:, a] = product.astype(jnp.bfloat16).reshape(chunks, chunk_rows, red)
        return carry

    lax.fori_loop(0, 1, weights, 0)
    pl.semaphore_wait(barrier, boxes_axis - 1 + groups - 1 + 2)

    def weights_sent(a, carry):
        send_w(0, a)

        @pl.when(a + 1 < box_count)
        def _():
            weights(a + 1, 0)

        return carry

    lax.fori_loop(0, box_count, weights_sent, 0)
    for copy in load_own:
        copy.wait()
    taken = [0, 0]
    for a in range(box_count):
        for j in range(slots):
            i = a * slots + j
            owner = near_s[a, j] // box_count
            place = (near_s[a, j] - owner * box_count) * slots + slot_s[a, j]
            asked = [owner == after, owner == behind]
            list_s[2, 0, i] = jnp.where(jnp.logical_or(asked[0], asked[1]), total, place)
            list_s[2, 1, i] = jnp.where(asked[0], taken[0], jnp.where(asked[1], FAR + taken[1], 2 * FAR))
            place_s[i] = place
            for d in range(2):
                asked_s[d, i] = jnp.where(asked[d], taken[d], -1)
                taken[d] = taken[d] + jnp.where(asked[d], 1, 0)

    def request(k, carry):
        for d in range(2):
            found_tile, found_box = 0, 0
            for i in range(total):
                match = asked_s[d, i] == k
                found_tile = found_tile + jnp.where(match, place_s[i], 0)
                found_box = found_box + jnp.where(match, i // slots, 0)
            list_s[d, 0, k] = found_tile
            list_s[d, 1, k] = found_box
        return carry

    lax.fori_loop(0, FAR, request, 0)
    to_vectors = pltpu.make_async_copy(list_s.at[pl.ds(0, 2)], list_out, load_sem.at[box_count + 3])
    to_vectors.start()
    to_vectors.wait()
    list_copies = [
        pltpu.make_async_remote_copy(
            src_ref=list_out.at[d],
            dst_ref=list_in.at[1 - d],
            send_sem=list_send.at[d],
            recv_sem=list_recv.at[1 - d],
            device_id=beside[d],
            device_id_type=MESH,
        )
        for d in range(2)
    ]
    for copy in list_copies:
        copy.start()


    load_full.wait()
    load_tiles.wait()
    for q, dx in pieces:
        load_near(q, dx).wait()

    def local_terms(a, carry):
        w = own_w[:, a].reshape(skel, red)
        own = lax.dot_general(w, full_c[a], (((1,), (1,)), ((), ())), preferred_element_type=jnp.float32)
        cols = pl.ds(0, skel)
        near = base[:, a, :, cols].reshape(skel, skel).astype(jnp.float32)
        base[:, a, :, cols] = (near - own).astype(jnp.bfloat16).reshape(chunks, chunk_rows, skel)
        for j in range(slots):
            cols = pl.ds((j + 1) * skel, skel)
            pair = jnp.dot(w, tile[jnp.clip(list_s[2, 0, a * slots + j], 0, total)], preferred_element_type=jnp.float32)
            near = base[:, a, :, cols].reshape(skel, skel).astype(jnp.float32)
            base[:, a, :, cols] = (near - pair).astype(jnp.bfloat16).reshape(chunks, chunk_rows, skel)
        return carry

    lax.fori_loop(0, box_count, local_terms, 0)
    send_w_all(1)

    for copy in list_copies:
        copy.wait()
    to_scalars = pltpu.make_async_copy(list_in, list_s.at[pl.ds(0, 2)], load_sem.at[box_count + 2])
    to_scalars.start()
    to_scalars.wait()

    def remote_terms(q):
        for d in range(2):
            pltpu.make_async_copy(wr[q].at[d], wr[q].at[d], w_recv.at[q, d]).wait()

        def one(n, carry):
            for d in range(2):
                for i in range(GROUP):
                    k = n * GROUP + i
                    asked_box = jnp.clip(list_s[d, 1, k], 0, box_count - 1)
                    asked_tile = jnp.clip(list_s[d, 0, k], 0, total)
                    pair = jnp.dot(wr[q][d, asked_box], tile[asked_tile], preferred_element_type=jnp.float32)
                    rs[q][d, k] = pair.astype(jnp.bfloat16)
                pltpu.make_async_remote_copy(
                    src_ref=rs[q].at[d, pl.ds(n * GROUP, GROUP)],
                    dst_ref=res[q].at[pl.ds((1 - d) * FAR + n * GROUP, GROUP)],
                    send_sem=r_send.at[q, d],
                    recv_sem=r_recv.at[q, 1 - d],
                    device_id=beside[d],
                    device_id_type=MESH,
                ).start()
            return carry

        lax.fori_loop(0, FAR // GROUP, one, 0)

    def finish(q):
        for d in range(2):
            arrived = res[q].at[pl.ds(d * FAR, FAR)]
            pltpu.make_async_copy(arrived, arrived, r_recv.at[q, d]).wait()

        def one(a, carry):
            ob[q][:, a, :, pl.ds(0, skel)] = base[q, a, :, pl.ds(0, skel)].reshape(dests, 8, skel)
            for j in range(slots):
                cols = pl.ds((j + 1) * skel, skel)
                arrived = res[q][jnp.clip(list_s[2, 1, a * slots + j], 0, 2 * FAR)]
                value = base[q, a, :, cols].astype(jnp.float32) - arrived.astype(jnp.float32)
                ob[q][:, a, :, cols] = value.reshape(dests, 8, skel).astype(jnp.bfloat16)
            return carry

        lax.fori_loop(0, box_count, one, 0)

        def send(s, carry):
            dx, to_c = s % groups, lax.rem(c + s // groups, 2)
            to_x, to_z = to_xz(q, dx)
            pltpu.make_async_remote_copy(
                src_ref=ob[q].at[dx * 2 + to_c],
                dst_ref=stage.at[x, z, c],
                send_sem=st_send.at[q],
                recv_sem=st_recv.at[q, x],
                device_id=(to_x * per_group + to_z * 2 + to_c, g),
                device_id_type=MESH,
            ).start()
            return carry

        if q == 0:
            pltpu.make_async_copy(ob[q].at[c], stage.at[x, z, c], st_recv.at[q, x]).start()
        lax.fori_loop(1 if q == 0 else 0, dests, send, 0)

    def forward(q):
        for step in (0, 1, 3, 2):
            from_x = lax.rem(x + step, groups)
            from_z = lax.rem(z - q + lax.rem(groups - step, groups) + 2 * z_count, z_count)
            piece = stage.at[from_x, from_z]
            pltpu.make_async_copy(piece, piece, st_recv.at[q, from_x]).wait()
            place = out.at[from_z, :, g]

            @pl.when(from_x == g)
            def _():
                pltpu.make_async_copy(piece, place, out_recv).start()

            @pl.when(from_x != g)
            def _():
                pltpu.make_async_remote_copy(
                    src_ref=piece,
                    dst_ref=place,
                    send_sem=out_send.at[q],
                    recv_sem=out_recv,
                    device_id=(b, from_x),
                    device_id_type=MESH,
                ).start()

    for step, q in (
        (remote_terms, 0), (send_w_all, 2), (remote_terms, 1), (send_w_all, 3), (finish, 0), (remote_terms, 2),
        (finish, 1), (forward, 0), (remote_terms, 3), (finish, 2), (forward, 1), (finish, 3), (forward, 2), (forward, 3),
    ):
        step(q)

    pltpu.make_async_copy(out, out, out_recv).wait()
    for q in range(chunks):
        for d in range(2):
            pltpu.make_async_copy(wr[q].at[d], wr[q].at[d], w_send.at[q, d]).wait()
            pltpu.make_async_copy(rs[q].at[d], rs[q].at[d], r_send.at[q, d]).wait()
        sent = ob[q].at[pl.ds(0, dests - 1 if q == 0 else dests)]
        pltpu.make_async_copy(sent, sent, st_send.at[q]).wait()
        sent = stage.at[pl.ds(0, groups - 1), 0]
        pltpu.make_async_copy(sent, sent, out_send.at[q]).wait()


def per_device(groups, boxes_axis, coupling, inverse, tiles, near_block, neighbour, source_slot):
    box_count, skel, red = coupling.shape
    slots = neighbour.shape[1]
    total = box_count * slots
    width = near_block.shape[-1]
    rows = skel // boxes_axis
    chunks = boxes_axis // groups // 2
    chunk_rows = skel // chunks
    half = jnp.bfloat16
    split = (box_count, groups, chunks, 2 * rows)
    hbm = pl.BlockSpec(memory_space=pl.ANY)
    big = (neighbour, source_slot, coupling.reshape(split + (red,)), coupling, inverse, tiles.reshape(total, red, skel), near_block.reshape(split + (width,)))
    big = [pltpu.with_memory_space_constraint(array, pltpu.HBM) for array in big]
    moved = pl.pallas_call(
        functools.partial(kernel, groups, boxes_axis, chunks, slots),
        out_shape=pltpu.VMEM((chunks, 2, groups, box_count, rows, width), half),
        in_specs=[hbm] * 7,
        out_specs=pl.BlockSpec(memory_space=pl.ANY),
        scratch_shapes=[
            pltpu.VMEM((box_count, skel, red), half),
            pltpu.VMEM((box_count, red, red), half),
            pltpu.VMEM((box_count, skel, red), half),
            pltpu.VMEM((total + 1, red, skel), half),
            pltpu.VMEM((chunks, box_count, chunk_rows, width), half),
            pltpu.VMEM((chunks, box_count, chunk_rows, red), half),
            pltpu.VMEM((groups, chunks, 2, box_count, rows, width), half),
            pltpu.VMEM((2, 8, 128), jnp.int32),
            pltpu.VMEM((2, 8, 128), jnp.int32),
            pltpu.SMEM((3, 8, 128), jnp.int32),
            pltpu.SMEM((2, total), jnp.int32),
            pltpu.SMEM((total,), jnp.int32),
            pltpu.SMEM(neighbour.shape, jnp.int32),
            pltpu.SMEM(neighbour.shape, jnp.int32),
            pltpu.SemaphoreType.DMA((box_count + 5,)),
            pltpu.SemaphoreType.DMA((chunks * groups,)),
            pltpu.SemaphoreType.DMA((chunks * groups,)),
            pltpu.SemaphoreType.DMA((2,)),
            pltpu.SemaphoreType.DMA((2,)),
            pltpu.SemaphoreType.DMA((chunks, 2)),
            pltpu.SemaphoreType.DMA((chunks, 2)),
            pltpu.SemaphoreType.DMA((chunks, 2)),
            pltpu.SemaphoreType.DMA((chunks, 2)),
            pltpu.SemaphoreType.DMA((chunks,)),
            pltpu.SemaphoreType.DMA((chunks, groups)),
            pltpu.SemaphoreType.DMA((chunks,)),
            pltpu.SemaphoreType.DMA,
        ]
        + [pltpu.VMEM((2, box_count, chunk_rows, red), half)] * chunks
        + [pltpu.VMEM((2, FAR, chunk_rows, skel), half)] * chunks
        + [pltpu.VMEM((2 * FAR + 1, chunk_rows, skel), half)] * chunks
        + [pltpu.VMEM((2 * groups, box_count, rows, width), half)] * chunks,
        compiler_params=pltpu.CompilerParams(
            collective_id=0, has_side_effects=True, vmem_limit_bytes=48 * 2**20
        ),
        cost_estimate=pl.CostEstimate(flops=9 * 10**9, bytes_accessed=24 * 10**6, transcendentals=0),
    )(
        *big,
    )
    return moved.reshape(-1, rows, width)


def solution(mesh):
    return jax.shard_map(
        functools.partial(per_device, mesh.shape["grp"], mesh.shape["box"]),
        mesh=mesh,
        in_specs=(
            P(("box", "grp"), None, None),
            P(("box", "grp"), None, None),
            P(("box", "grp"), None, None, None),
            P(("box", "grp"), None, None),
            P(("box", "grp"), None),
            P(("box", "grp"), None),
        ),
        out_specs=P("grp", "box", None),
        check_vma=False,
    )
```

```python
import functools

import jax
import jax.numpy as jnp
from jax import lax
from jax.experimental import pallas as pl
from jax.experimental.pallas import tpu as pltpu
from jax.sharding import PartitionSpec as P

FAR = 12
GROUP = 3
MESH = pl.DeviceIdType.MESH


def kernel(
    groups, boxes_axis, chunks, slots,
    neighbour, source_slot, split_coupling, coupling, inverse, tiles, split_near,
    out,
    cp, inv, full_c, tile, base, own_w, stage, list_out, list_in, list_s, asked_s, place_s, near_s, slot_s,
    load_sem, c_sem, near_sem, list_send, list_recv, w_send, w_recv, r_send, r_recv,
    st_send, st_recv, out_send, out_recv, *buffers,
):
    box_count, skel, red = cp.shape
    total = box_count * slots
    per_group = boxes_axis // groups
    z_count = chunks
    piece_rows = 16
    chunk_rows = groups * piece_rows
    dests = groups * 2
    wr, rs, res, ob = (buffers[n * chunks : (n + 1) * chunks] for n in range(4))
    b = lax.axis_index("box")
    g = lax.axis_index("grp")
    x = b // per_group
    z = (b % per_group) // 2
    c = b % 2
    count = boxes_axis * groups
    here = b * groups + g
    after = lax.rem(here + 1, count)
    behind = lax.rem(here + count - 1, count)
    beside = ((after // groups, after % groups), (behind // groups, behind % groups))

    def to_xz(q, dx):
        return lax.rem(x + dx, groups), lax.rem(z + q - dx + 2 * z_count, z_count)

    def load_c(q, dx):
        to_x, to_z = to_xz(q, dx)
        rows = pl.ds((q * groups + dx) * piece_rows, piece_rows)
        return pltpu.make_async_copy(split_coupling.at[:, to_x, to_z], cp.at[:, rows], c_sem.at[q * groups + dx])

    def load_near(q, dx):
        to_x, to_z = to_xz(q, dx)
        rows = pl.ds(dx * piece_rows, piece_rows)
        return pltpu.make_async_copy(
            split_near.at[:, to_x, to_z], base.at[q, :, rows], near_sem.at[q * groups + dx]
        )

    def load_inv(a):
        return pltpu.make_async_copy(inverse.at[a], inv.at[a], load_sem.at[a])

    pieces = [(q, dx) for q in range(chunks) for dx in range(groups)]
    for q, dx in pieces:
        load_c(q, dx).start()
    for a in range(box_count):
        load_inv(a).start()
    barrier = pltpu.get_barrier_semaphore()

    def greet(k, carry):
        pl.semaphore_signal(barrier, inc=1, device_id=(lax.rem(b + k, boxes_axis), g), device_id_type=MESH)
        return carry

    lax.fori_loop(1, boxes_axis, greet, 0)
    for k in range(1, groups):
        pl.semaphore_signal(barrier, inc=1, device_id=(b, lax.rem(g + k, groups)), device_id_type=MESH)
    for device in beside:
        pl.semaphore_signal(barrier, inc=1, device_id=device, device_id_type=MESH)

    load_tiles = pltpu.make_async_copy(tiles, tile.at[pl.ds(0, total)], load_sem.at[box_count])
    load_full = pltpu.make_async_copy(coupling, full_c, load_sem.at[box_count + 1])
    load_own = [
        pltpu.make_async_copy(neighbour, near_s, load_sem.at[box_count + 2]),
        pltpu.make_async_copy(source_slot, slot_s, load_sem.at[box_count + 4]),
    ]
    load_full.start()
    load_tiles.start()
    for q, dx in pieces:
        load_near(q, dx).start()
    for copy in load_own:
        copy.start()
    tile[total] = jnp.zeros_like(tile[total])
    for q in range(chunks):
        res[q][2 * FAR] = jnp.zeros_like(res[q][2 * FAR])

    def send_w(q, a):
        for d in range(2):
            pltpu.make_async_remote_copy(
                src_ref=own_w.at[q, a],
                dst_ref=wr[q].at[1 - d, a],
                send_sem=w_send.at[q, d],
                recv_sem=w_recv.at[q, 1 - d],
                device_id=beside[d],
                device_id_type=MESH,
            ).start()

    def send_w_all(q):
        for d in range(2):
            pltpu.make_async_remote_copy(
                src_ref=own_w.at[q],
                dst_ref=wr[q].at[1 - d],
                send_sem=w_send.at[q, d],
                recv_sem=w_recv.at[q, 1 - d],
                device_id=beside[d],
                device_id_type=MESH,
            ).start()

    for dx in range(groups):
        load_c(0, dx).wait()

    def weights(a, carry):
        load_inv(a).wait()
        product = jnp.dot(cp[a, pl.ds(0, chunk_rows)], inv[a], preferred_element_type=jnp.float32)
        own_w[0, a] = product.astype(jnp.bfloat16)
        return carry

    def later_weights(a, carry):
        rows = pl.ds(chunk_rows, skel - chunk_rows)
        product = jnp.dot(cp[a, rows], inv[a], preferred_element_type=jnp.float32)
        own_w[pl.ds(1, chunks - 1), a] = product.astype(jnp.bfloat16).reshape(chunks - 1, chunk_rows, red)
        return carry

    lax.fori_loop(0, 1, weights, 0)
    pl.semaphore_wait(barrier, boxes_axis - 1 + groups - 1 + 2)

    def weights_sent(a, carry):
        send_w(0, a)

        @pl.when(a + 1 < box_count)
        def _():
            weights(a + 1, 0)

        return carry

    lax.fori_loop(0, box_count, weights_sent, 0)
    for q, dx in pieces[groups:]:
        load_c(q, dx).wait()
    lax.fori_loop(0, box_count, later_weights, 0)
    for copy in load_own:
        copy.wait()
    taken = [0, 0]
    for a in range(box_count):
        for j in range(slots):
            i = a * slots + j
            owner = near_s[a, j] // box_count
            place = (near_s[a, j] - owner * box_count) * slots + slot_s[a, j]
            asked = [owner == after, owner == behind]
            list_s[2, 0, i] = jnp.where(jnp.logical_or(asked[0], asked[1]), total, place)
            list_s[2, 1, i] = jnp.where(asked[0], taken[0], jnp.where(asked[1], FAR + taken[1], 2 * FAR))
            place_s[i] = place
            for d in range(2):
                asked_s[d, i] = jnp.where(asked[d], taken[d], -1)
                taken[d] = taken[d] + jnp.where(asked[d], 1, 0)

    def request(k, carry):
        for d in range(2):
            found_tile, found_box = 0, 0
            for i in range(total):
                match = asked_s[d, i] == k
                found_tile = found_tile + jnp.where(match, place_s[i], 0)
                found_box = found_box + jnp.where(match, i // slots, 0)
            list_s[d, 0, k] = found_tile
            list_s[d, 1, k] = found_box
        return carry

    lax.fori_loop(0, FAR, request, 0)
    to_vectors = pltpu.make_async_copy(list_s.at[pl.ds(0, 2)], list_out, load_sem.at[box_count + 3])
    to_vectors.start()
    to_vectors.wait()
    list_copies = [
        pltpu.make_async_remote_copy(
            src_ref=list_out.at[d],
            dst_ref=list_in.at[1 - d],
            send_sem=list_send.at[d],
            recv_sem=list_recv.at[1 - d],
            device_id=beside[d],
            device_id_type=MESH,
        )
        for d in range(2)
    ]
    for copy in list_copies:
        copy.start()


    load_full.wait()
    load_tiles.wait()
    for q, dx in pieces:
        load_near(q, dx).wait()

    def local_terms(a, carry):
        w = own_w[:, a].reshape(skel, red)
        own = lax.dot_general(w, full_c[a], (((1,), (1,)), ((), ())), preferred_element_type=jnp.float32)
        cols = pl.ds(0, skel)
        near = base[:, a, :, cols].reshape(skel, skel).astype(jnp.float32)
        base[:, a, :, cols] = (near - own).astype(jnp.bfloat16).reshape(chunks, chunk_rows, skel)
        for j in range(slots):
            cols = pl.ds((j + 1) * skel, skel)
            pair = jnp.dot(w, tile[jnp.clip(list_s[2, 0, a * slots + j], 0, total)], preferred_element_type=jnp.float32)
            near = base[:, a, :, cols].reshape(skel, skel).astype(jnp.float32)
            base[:, a, :, cols] = (near - pair).astype(jnp.bfloat16).reshape(chunks, chunk_rows, skel)
        return carry

    lax.fori_loop(0, box_count, local_terms, 0)
    send_w_all(1)

    for copy in list_copies:
        copy.wait()
    to_scalars = pltpu.make_async_copy(list_in, list_s.at[pl.ds(0, 2)], load_sem.at[box_count + 2])
    to_scalars.start()
    to_scalars.wait()

    def remote_terms(q):
        for d in range(2):
            pltpu.make_async_copy(wr[q].at[d], wr[q].at[d], w_recv.at[q, d]).wait()

        def one(n, carry):
            for d in range(2):
                for i in range(GROUP):
                    k = n * GROUP + i
                    asked_box = jnp.clip(list_s[d, 1, k], 0, box_count - 1)
                    asked_tile = jnp.clip(list_s[d, 0, k], 0, total)
                    pair = jnp.dot(wr[q][d, asked_box], tile[asked_tile], preferred_element_type=jnp.float32)
                    rs[q][d, k] = pair.astype(jnp.bfloat16)
                pltpu.make_async_remote_copy(
                    src_ref=rs[q].at[d, pl.ds(n * GROUP, GROUP)],
                    dst_ref=res[q].at[pl.ds((1 - d) * FAR + n * GROUP, GROUP)],
                    send_sem=r_send.at[q, d],
                    recv_sem=r_recv.at[q, 1 - d],
                    device_id=beside[d],
                    device_id_type=MESH,
                ).start()
            return carry

        lax.fori_loop(0, FAR // GROUP, one, 0)

    def finish(q):
        for d in range(2):
            arrived = res[q].at[pl.ds(d * FAR, FAR)]
            pltpu.make_async_copy(arrived, arrived, r_recv.at[q, d]).wait()

        def one(a, carry):
            ob[q][:, a, :, pl.ds(0, skel)] = base[q, a, :, pl.ds(0, skel)].reshape(dests, 8, skel)
            for j in range(slots):
                cols = pl.ds((j + 1) * skel, skel)
                arrived = res[q][jnp.clip(list_s[2, 1, a * slots + j], 0, 2 * FAR)]
                value = base[q, a, :, cols].astype(jnp.float32) - arrived.astype(jnp.float32)
                ob[q][:, a, :, cols] = value.reshape(dests, 8, skel).astype(jnp.bfloat16)
            return carry

        lax.fori_loop(0, box_count, one, 0)

        def send(s, carry):
            dx, to_c = s % groups, lax.rem(c + s // groups, 2)
            to_x, to_z = to_xz(q, dx)
            pltpu.make_async_remote_copy(
                src_ref=ob[q].at[dx * 2 + to_c],
                dst_ref=stage.at[x, z, c],
                send_sem=st_send.at[q],
                recv_sem=st_recv.at[q, x],
                device_id=(to_x * per_group + to_z * 2 + to_c, g),
                device_id_type=MESH,
            ).start()
            return carry

        if q == 0:
            pltpu.make_async_copy(ob[q].at[c], stage.at[x, z, c], st_recv.at[q, x]).start()
        lax.fori_loop(1 if q == 0 else 0, dests, send, 0)

    def forward(q):
        for step in (0, 1, 3, 2):
            from_x = lax.rem(x + step, groups)
            from_z = lax.rem(z - q + lax.rem(groups - step, groups) + 2 * z_count, z_count)
            piece = stage.at[from_x, from_z]
            pltpu.make_async_copy(piece, piece, st_recv.at[q, from_x]).wait()
            place = out.at[from_z, :, g]

            @pl.when(from_x == g)
            def _():
                pltpu.make_async_copy(piece, place, out_recv).start()

            @pl.when(from_x != g)
            def _():
                pltpu.make_async_remote_copy(
                    src_ref=piece,
                    dst_ref=place,
                    send_sem=out_send.at[q],
                    recv_sem=out_recv,
                    device_id=(b, from_x),
                    device_id_type=MESH,
                ).start()

    for step, q in (
        (remote_terms, 0), (send_w_all, 2), (remote_terms, 1), (send_w_all, 3), (finish, 0), (remote_terms, 2),
        (finish, 1), (forward, 0), (remote_terms, 3), (finish, 2), (forward, 1), (finish, 3), (forward, 2), (forward, 3),
    ):
        step(q)

    pltpu.make_async_copy(out, out, out_recv).wait()
    for q in range(chunks):
        for d in range(2):
            pltpu.make_async_copy(wr[q].at[d], wr[q].at[d], w_send.at[q, d]).wait()
            pltpu.make_async_copy(rs[q].at[d], rs[q].at[d], r_send.at[q, d]).wait()
        sent = ob[q].at[pl.ds(0, dests - 1 if q == 0 else dests)]
        pltpu.make_async_copy(sent, sent, st_send.at[q]).wait()
        sent = stage.at[pl.ds(0, groups - 1), 0]
        pltpu.make_async_copy(sent, sent, out_send.at[q]).wait()


def per_device(groups, boxes_axis, coupling, inverse, tiles, near_block, neighbour, source_slot):
    box_count, skel, red = coupling.shape
    slots = neighbour.shape[1]
    total = box_count * slots
    width = near_block.shape[-1]
    rows = skel // boxes_axis
    chunks = boxes_axis // groups // 2
    chunk_rows = skel // chunks
    half = jnp.bfloat16
    split = (box_count, groups, chunks, 2 * rows)
    hbm = pl.BlockSpec(memory_space=pl.ANY)
    big = (neighbour, source_slot, coupling.reshape(split + (red,)), coupling, inverse, tiles.reshape(total, red, skel), near_block.reshape(split + (width,)))
    big = [pltpu.with_memory_space_constraint(array, pltpu.HBM) for array in big]
    moved = pl.pallas_call(
        functools.partial(kernel, groups, boxes_axis, chunks, slots),
        out_shape=pltpu.VMEM((chunks, 2, groups, box_count, rows, width), half),
        in_specs=[hbm] * 7,
        out_specs=pl.BlockSpec(memory_space=pl.ANY),
        scratch_shapes=[
            pltpu.VMEM((box_count, skel, red), half),
            pltpu.VMEM((box_count, red, red), half),
            pltpu.VMEM((box_count, skel, red), half),
            pltpu.VMEM((total + 1, red, skel), half),
            pltpu.VMEM((chunks, box_count, chunk_rows, width), half),
            pltpu.VMEM((chunks, box_count, chunk_rows, red), half),
            pltpu.VMEM((groups, chunks, 2, box_count, rows, width), half),
            pltpu.VMEM((2, 8, 128), jnp.int32),
            pltpu.VMEM((2, 8, 128), jnp.int32),
            pltpu.SMEM((3, 8, 128), jnp.int32),
            pltpu.SMEM((2, total), jnp.int32),
            pltpu.SMEM((total,), jnp.int32),
            pltpu.SMEM(neighbour.shape, jnp.int32),
            pltpu.SMEM(neighbour.shape, jnp.int32),
            pltpu.SemaphoreType.DMA((box_count + 5,)),
            pltpu.SemaphoreType.DMA((chunks * groups,)),
            pltpu.SemaphoreType.DMA((chunks * groups,)),
            pltpu.SemaphoreType.DMA((2,)),
            pltpu.SemaphoreType.DMA((2,)),
            pltpu.SemaphoreType.DMA((chunks, 2)),
            pltpu.SemaphoreType.DMA((chunks, 2)),
            pltpu.SemaphoreType.DMA((chunks, 2)),
            pltpu.SemaphoreType.DMA((chunks, 2)),
            pltpu.SemaphoreType.DMA((chunks,)),
            pltpu.SemaphoreType.DMA((chunks, groups)),
            pltpu.SemaphoreType.DMA((chunks,)),
            pltpu.SemaphoreType.DMA,
        ]
        + [pltpu.VMEM((2, box_count, chunk_rows, red), half)] * chunks
        + [pltpu.VMEM((2, FAR, chunk_rows, skel), half)] * chunks
        + [pltpu.VMEM((2 * FAR + 1, chunk_rows, skel), half)] * chunks
        + [pltpu.VMEM((2 * groups, box_count, rows, width), half)] * chunks,
        compiler_params=pltpu.CompilerParams(
            collective_id=0, has_side_effects=True, vmem_limit_bytes=48 * 2**20
        ),
        cost_estimate=pl.CostEstimate(flops=9 * 10**9, bytes_accessed=24 * 10**6, transcendentals=0),
    )(
        *big,
    )
    return moved.reshape(-1, rows, width)


def solution(mesh):
    return jax.shard_map(
        functools.partial(per_device, mesh.shape["grp"], mesh.shape["box"]),
        mesh=mesh,
        in_specs=(
            P(("box", "grp"), None, None),
            P(("box", "grp"), None, None),
            P(("box", "grp"), None, None, None),
            P(("box", "grp"), None, None),
            P(("box", "grp"), None),
            P(("box", "grp"), None),
        ),
        out_specs=P("grp", "box", None),
        check_vma=False,
    )
```
